32 devices in a mesh: dom: 2 (over y), row: 4 (over z), feat: 4 (over x, core).
Axes of the slice: x: 2, y: 2, z: 4, core: 2. Of those that a mesh axis runs over, the one named last changes fastest.
Arguments:
- feats: bfloat16 [65536, 768], P(('dom', 'row'), 'feat'), parts along dimension 0, may hold values from -6 to 6
- req_rows: int32 [8, 1536], P(('dom', 'row')), parts along dimension 0, may hold values from 0 to 8191
- req_slots: int32 [8, 1536], P(('dom', 'row')), parts along dimension 0, may hold values from 0 to 3199
- block_count: int32 [8, 4], P(('dom', 'row')), parts along dimension 0, may hold values from 1 to 3, as said below
- rel_weight: bfloat16 [6, 768, 1024], P(None, 'feat'), may hold values from -0.21875 to 0.21875
- bias: float32 [1024], replicated, may hold values from -3 to 3
- gain: float32 [1024], replicated, may hold values from 0.5 to 1.5
- offset: float32 [1024], replicated, may hold values from -3 to 3
Outputs:
- hidden: bfloat16 [5120, 1024], P(('dom', 'row', 'feat')), parts along dimension 0
The draws below stay inside these ranges and needn't reach their ends.
There are 2 independent parts, one for each index of `dom`. The reference program is written for one: setup_inputs(seed, part) draws one part's arguments, and reference() takes and returns one part's arrays. A program takes and returns all parts, laid end to end along the dimension named above; an argument that names none is the same for every part. Nothing has to cross between parts.
Inputs may be any that keep to these rules, and one draw needn't show every extreme that they name: `req_rows`: a row index on the owner of its block. `req_slots`: t * 5 + r for a target t of the asking device and a relation r. Only the first block_count * 128 of the 384 slots a device keeps for an owner are live; in every draw some owner receives 3 blocks from every device.
All inputs are finite; a program needn't handle non-finite values.
Results may differ from the reference program's by a relative error of at most 0.0019.
Values may be sent and summed in bfloat16 or wider, within the bound.
A program may use at most 128 MiB of HBM per device.

```python
import jax
import jax.numpy as jnp
from jax import lax

F = 768
H = 1024
REL = 5
BLK = 128
SLOTS = 3
TGT_DEV = 640
NODE_DEV = 8192
NODES = 32768
TARGETS = 2560
REQ = 1536
N_ROW = 4


def draw_block_count(key, part):
    key = jax.random.fold_in(key, 7)
    base_key, hot_key = jax.random.split(key)
    base = jax.random.randint(base_key, (N_ROW, N_ROW), 1, SLOTS)
    order = jax.random.permutation(hot_key, N_ROW)
    hot_owner = order < max(1, N_ROW // 8)
    return jnp.where(hot_owner[None, :], SLOTS, base).astype(jnp.int32)


def plant(array, stream_key, low, top_value):
    shape = array.shape
    place = [jax.random.randint(jax.random.fold_in(stream_key, axis), (), 0, shape[axis]) for axis in range(len(shape))]
    array = array.at[tuple(place)].set(low)
    longest = shape.index(max(shape))
    place[longest] = (place[longest] + 1) % shape[longest]
    return array.at[tuple(place)].set(top_value)


def levels(own_key, shape, cuts, least, top_value):
    def one(position, shards_of):
        steps = jax.random.uniform(jax.random.fold_in(jax.random.fold_in(own_key, 6), position), (shards_of,), jnp.float32, least / len(cuts), top_value / len(cuts))
        return jnp.repeat(jnp.exp(steps), shape[position] // shards_of).reshape((-1,) + (1,) * (len(shape) - position - 1))

    level = one(*cuts[0])
    for cut in cuts[1:]:
        level = level * one(*cut)
    return level


def gaussian(stream_key, shape, scale, bound, pieces=(), kind=jnp.bfloat16):
    drawn = scale * jax.random.normal(stream_key, shape, jnp.float32)
    if pieces:
        drawn = drawn * levels(stream_key, shape, pieces, -0.22, 0.18)
    return jnp.clip(drawn, -bound, bound).astype(kind)


def setup_inputs(seed: int = 0, part: int = 0) -> dict:
    streams_of = jax.random.split(jax.random.key(seed), 9)
    part_keys = jax.random.split(jax.random.fold_in(streams_of[8], part), 9)
    feats = gaussian(part_keys[0], (NODES, F), 1.0, 6.0, ((0, 4), (1, 4)))
    req_rows = plant(jax.random.randint(part_keys[1], (N_ROW, REQ), 0, NODE_DEV), jax.random.fold_in(part_keys[1], 1), 0, NODE_DEV - 1).astype(jnp.int32)
    req_slots = plant(jax.random.randint(part_keys[2], (N_ROW, REQ), 0, TGT_DEV * REL), jax.random.fold_in(part_keys[2], 1), 0, (TGT_DEV * REL) - 1).astype(jnp.int32)
    block_count = draw_block_count(jax.random.fold_in(jax.random.fold_in(streams_of[8], part), 71), part)
    rel_weight = gaussian(streams_of[4], (REL + 1, F, H), F ** -0.5, 0.21875, ((1, 4),))
    bias = gaussian(streams_of[5], (H,), 0.5, 3.0, (), jnp.float32)
    gain = jnp.clip(1.0 + 0.1 * jax.random.normal(streams_of[6], (H,), jnp.float32), 0.5, 1.5)
    offset = gaussian(streams_of[7], (H,), 0.5, 3.0, (), jnp.float32)
    return dict(feats=feats, req_rows=req_rows, req_slots=req_slots, block_count=block_count, rel_weight=rel_weight, bias=bias, gain=gain, offset=offset)


epsilon = 1e-05

def reference(feats, req_rows, req_slots, block_count, rel_weight, bias, gain, offset):
    flat_weight = rel_weight.reshape((REL + 1) * F, H)
    owner_base = jnp.arange(N_ROW, dtype=jnp.int32) * NODE_DEV
    slot_pos = jnp.arange(SLOTS * BLK, dtype=jnp.int32)

    def one_device(dest):
        rows = req_rows[dest].reshape(N_ROW, SLOTS * BLK) + owner_base[:, None]
        fetched = jnp.take(feats, rows.reshape(-1), axis=0)
        live_slots = (slot_pos[None, :] < block_count[dest][:, None] * BLK).reshape(-1).astype(jnp.float32)
        segments = req_slots[dest]
        counts = jax.ops.segment_sum(live_slots, segments, num_segments=TGT_DEV * REL)
        weights_slot = live_slots / jnp.maximum(counts, 1.0)[segments]
        summed = jax.ops.segment_sum(fetched.astype(jnp.float32) * weights_slot[:, None], segments, num_segments=TGT_DEV * REL)
        mean_rows = summed.astype(jnp.bfloat16).reshape(TGT_DEV, REL * F)
        own_rows = lax.dynamic_slice_in_dim(feats, (dest * NODE_DEV).astype(jnp.int32), TGT_DEV, 0)
        operand = jnp.concatenate([mean_rows, own_rows], axis=1)
        projected = jnp.dot(operand, flat_weight, preferred_element_type=jnp.float32) + bias
        activated = jnp.maximum(projected, 0.0)
        row_mean = lax.optimization_barrier(jnp.mean(activated, axis=1, keepdims=True))
        deviation = activated - row_mean
        row_spread = lax.optimization_barrier(jnp.mean(deviation * deviation, axis=1, keepdims=True))
        return (deviation * lax.rsqrt(row_spread + epsilon) * gain + offset).astype(jnp.bfloat16)
    result = lax.map(one_device, jnp.arange(N_ROW, dtype=jnp.int32))
    return result.reshape(TARGETS, H)
```

```python
import functools

import jax
import jax.numpy as jnp
from jax import lax
from jax.experimental import pallas as pl
from jax.experimental.pallas import tpu as pltpu
from jax.sharding import PartitionSpec as P

REL = 5
BLK = 128
MESH = pl.DeviceIdType.MESH
F32 = jnp.float32
BF16 = jnp.bfloat16

epsilon = 1e-05

FEAT_CHUNKS = 8
CAST_ROWS = 256
GATHER_UNROLL = 16
COL_PIECES = 4


def kernel(
    owners, bc_ref, rows_ref, slots_ref, feats_ref, weight_ref, bias_ref, gain_ref, offset_ref,
    out_ref,
    asked, feats_v, feats_f, weight_v, found, sent, got, block, agg, own_term, operand,
    part, half_in, half_out, last_in,
    asked_send, asked_recv, feats_sem, weight_sem, own_sem, row_send, row_recv,
    pair_send, pair_recv, far_send, far_recv,
):
    me = lax.axis_index("row")
    place = lax.axis_index("feat")
    high, low = place // 2, place % 2
    pair = {"feat": high * 2 + 1 - low}
    far = {"feat": (1 - high) * 2 + low}
    nodes, columns = feats_v.shape
    asks = slots_ref.shape[1] // owners
    half = asks // 2
    steps = owners - 1
    rows_out, width = out_ref.shape
    piece = width // COL_PIECES

    def shift(step):
        return 1 + lax.rem(owners // 2 - 1 + step, steps)

    def dest_of(step):
        return lax.rem(me + shift(step), owners)

    def owner_of(step):
        return lax.rem(me - shift(step) + owners, owners)

    def my_rows(owner):
        return rows_ref.at[:, pl.ds(pl.multiple_of(owner * asks, BLK), asks)]

    chunk_rows = nodes // FEAT_CHUNKS

    def feats_copy(c):
        span = pl.ds(pl.multiple_of(c * chunk_rows, chunk_rows), chunk_rows)
        return pltpu.make_async_copy(feats_ref.at[span, :], feats_v.at[span, :], feats_sem.at[c])

    for c in range(FEAT_CHUNKS):
        feats_copy(c).start()
    own_copy = pltpu.make_async_copy(my_rows(me), asked.at[steps], own_sem)
    own_copy.start()
    weight_copy = pltpu.make_async_copy(weight_ref, weight_v, weight_sem)
    weight_copy.start()

    barrier = pltpu.get_barrier_semaphore()

    @pl.loop(0, steps)
    def _(step):
        pl.semaphore_signal(barrier, inc=1, device_id={"row": dest_of(step)}, device_id_type=MESH)

    pl.semaphore_signal(barrier, inc=1, device_id=pair, device_id_type=MESH)
    pl.semaphore_signal(barrier, inc=1, device_id=far, device_id_type=MESH)
    pl.semaphore_wait(barrier, steps + 2)

    def ask(step):
        owner = owner_of(step)
        return pltpu.make_async_remote_copy(
            src_ref=my_rows(owner), dst_ref=asked.at[step],
            send_sem=asked_send.at[step], recv_sem=asked_recv.at[step],
            device_id={"row": owner}, device_id_type=MESH,
        )

    def answer(step):
        return pltpu.make_async_remote_copy(
            src_ref=sent.at[step], dst_ref=got.at[step],
            send_sem=row_send.at[step], recv_sem=row_recv.at[step],
            device_id={"row": dest_of(step)}, device_id_type=MESH,
        )

    @pl.loop(0, steps)
    def _(step):
        ask(step).start()

    @pl.loop(0, FEAT_CHUNKS)
    def _(c):
        feats_copy(c).wait()

        @pl.loop(0, chunk_rows // CAST_ROWS)
        def _(i):
            span = pl.ds(pl.multiple_of(c * chunk_rows + i * CAST_ROWS, CAST_ROWS), CAST_ROWS)
            feats_f[span, :] = feats_v[span, :].astype(F32)

    def gather(step, put):
        @pl.loop(0, asks // GATHER_UNROLL)
        def _(g):
            base = pl.multiple_of(g * GATHER_UNROLL, GATHER_UNROLL)
            for u in range(GATHER_UNROLL):
                node = asked[step, 0, base + u]
                found[pl.ds(base + u, 1), :] = feats_f[pl.ds(node, 1), :]

        put(slice(0, asks), found[:, :BLK].astype(BF16))
        tail = columns - BLK
        first = found[pl.ds(0, half), BLK:columns]
        second = found[pl.ds(half, half), BLK:columns]
        put(slice(asks, asks + half), jnp.concatenate([first, second], axis=1).astype(BF16))

    @pl.loop(0, steps)
    def _(step):
        ask(step).wait_recv()

        def put(span, value):
            sent[step, span, :] = value

        gather(step, put)
        answer(step).start()

    own_copy.wait()

    def put_own(span, value):
        got[steps, span, :] = value

    gather(steps, put_own)

    weight_copy.wait()

    @pl.loop(0, 4)
    def _(c):
        span = pl.ds(pl.multiple_of(c * rows_out, rows_out), rows_out)
        own_term[c] = jnp.dot(feats_v[span, :], weight_v[REL], preferred_element_type=F32)

    lane = lax.broadcasted_iota(jnp.int32, (asks, BLK), 1)

    def unpack(step):
        block[:, :BLK] = got[step, :asks, :]
        tails = got[step, asks:, :].astype(F32)
        both = jnp.concatenate([tails, pltpu.roll(tails, BLK // 2, 1)], axis=0)
        block[:, BLK:] = jnp.where(lane == columns - BLK, 1.0, both).astype(BF16)

    pos = lax.broadcasted_iota(jnp.int32, (1, asks), 1)

    def keys_of(owner):
        keys = slots_ref[:, pl.ds(pl.multiple_of(owner * asks, BLK), asks)]
        return jnp.where(pos < bc_ref[0, owner] * BLK, keys, -1)

    target = lax.broadcasted_iota(jnp.int32, (rows_out, asks), 0) * REL

    def sums(keys, chunk, rel):
        hits = target == keys - (chunk * rows_out * REL + rel)
        pick = jnp.where(hits, 1.0, 0.0).astype(BF16)
        return jnp.dot(pick, block[...], preferred_element_type=F32)

    unpack(steps)
    own_keys = keys_of(me)

    @pl.loop(0, 4)
    def _(chunk):
        for rel in range(REL):
            agg[chunk, rel] = sums(own_keys, chunk, rel)

    @pl.loop(0, steps - 1)
    def _(step):
        answer(step).wait_recv()
        unpack(step)
        keys = keys_of(owner_of(step))

        @pl.loop(0, 4)
        def _(chunk):
            for rel in range(REL):
                agg[chunk, rel] += sums(keys, chunk, rel)

    answer(steps - 1).wait_recv()
    unpack(steps - 1)
    last_keys = keys_of(owner_of(steps - 1))

    def operands(chunk):
        for rel in range(REL):
            total = agg[chunk, rel] + sums(last_keys, chunk, rel)
            count = total[:, columns:columns + 1]
            mean = total[:, :columns] * (1.0 / jnp.maximum(count, 1.0))
            operand[rel] = mean.astype(BF16)

    def project(chunk, q):
        cols = slice(q * piece, (q + 1) * piece)
        value = own_term[chunk, :, cols]
        for rel in range(REL):
            value += jnp.dot(operand[rel], weight_v[rel, :, cols], preferred_element_type=F32)
        return value

    def to_pair(i, q):
        return pltpu.make_async_remote_copy(
            src_ref=part.at[i, q], dst_ref=half_in.at[i, q],
            send_sem=pair_send.at[i, q], recv_sem=pair_recv.at[i, q],
            device_id=pair, device_id_type=MESH,
        )

    def to_far(q):
        return pltpu.make_async_remote_copy(
            src_ref=half_out.at[q], dst_ref=last_in.at[q],
            send_sem=far_send.at[q], recv_sem=far_recv.at[q],
            device_id=far, device_id_type=MESH,
        )

    chunk = (1 - high) * 2 + 1 - low
    operands(chunk)
    for q in range(COL_PIECES):
        part[0, q] = project(chunk, q)
        to_pair(0, q).start()

    chunk = (1 - high) * 2 + low
    operands(chunk)
    for q in range(COL_PIECES):
        value = project(chunk, q)
        to_pair(0, q).wait_recv()
        half_out[q] = value + half_in[0, q]
        to_far(q).start()

    chunk = high * 2 + 1 - low
    operands(chunk)
    for q in range(COL_PIECES):
        part[1, q] = project(chunk, q)
        to_pair(1, q).start()

    chunk = high * 2 + low
    operands(chunk)
    for q in range(COL_PIECES):
        cols = slice(q * piece, (q + 1) * piece)
        value = project(chunk, q)
        to_pair(1, q).wait_recv()
        own_term[chunk, :, cols] = value + half_in[1, q] + bias_ref[:, cols]

    total = jnp.zeros((rows_out, 1), F32)
    for q in range(COL_PIECES):
        cols = slice(q * piece, (q + 1) * piece)
        to_far(q).wait_recv()
        act = jnp.maximum(own_term[chunk, :, cols] + last_in[q], 0.0)
        last_in[q] = act
        total += jnp.sum(act, axis=1, keepdims=True)
    mu = total / width
    spread = jnp.zeros((rows_out, 1), F32)
    for q in range(COL_PIECES):
        dev = last_in[q] - mu
        spread += jnp.sum(dev * dev, axis=1, keepdims=True)
    scale = lax.rsqrt(spread / width + epsilon)
    for q in range(COL_PIECES):
        cols = slice(q * piece, (q + 1) * piece)
        dev = last_in[q] - mu
        out_ref[:, cols] = (dev * scale * gain_ref[:, cols] + offset_ref[:, cols]).astype(BF16)

    @pl.loop(0, steps)
    def _(step):
        ask(step).wait_send()
        answer(step).wait_send()

    for q in range(COL_PIECES):
        to_pair(0, q).wait_send()
        to_pair(1, q).wait_send()
        to_far(q).wait_send()


def body(feats, req_rows, req_slots, block_count, rel_weight, bias, gain, offset):
    owners = lax.axis_size("row")
    ranks = lax.axis_size("feat")
    nodes, columns = feats.shape
    rels, _, width = rel_weight.shape
    asks = req_rows.shape[1] // owners
    steps = owners - 1
    rows_out = 640 // ranks
    piece = width // COL_PIECES
    packed = asks + asks // 2
    dma = pltpu.SemaphoreType.DMA
    vmem = pl.BlockSpec(memory_space=pltpu.VMEM)
    hbm = pl.BlockSpec(memory_space=pl.ANY)
    return pl.pallas_call(
        functools.partial(kernel, owners),
        out_shape=jax.ShapeDtypeStruct((rows_out, width), BF16),
        in_specs=[pl.BlockSpec(memory_space=pltpu.SMEM), hbm, vmem, hbm, hbm, vmem, vmem, vmem],
        out_specs=vmem,
        scratch_shapes=[
            pltpu.SMEM((owners, 1, asks), jnp.int32),
            pltpu.VMEM((nodes, columns), BF16),
            pltpu.VMEM((nodes, columns), F32),
            pltpu.VMEM((rels, columns, width), BF16),
            pltpu.VMEM((asks, columns), F32),
            pltpu.VMEM((steps, packed, BLK), BF16),
            pltpu.VMEM((owners, packed, BLK), BF16),
            pltpu.VMEM((asks, 2 * BLK), BF16),
            pltpu.VMEM((ranks, REL, rows_out, 2 * BLK), F32),
            pltpu.VMEM((ranks, rows_out, width), F32),
            pltpu.VMEM((REL, rows_out, columns), BF16),
            pltpu.VMEM((2, COL_PIECES, rows_out, piece), F32),
            pltpu.VMEM((2, COL_PIECES, rows_out, piece), F32),
            pltpu.VMEM((COL_PIECES, rows_out, piece), F32),
            pltpu.VMEM((COL_PIECES, rows_out, piece), F32),
            dma((steps,)), dma((steps,)), dma((FEAT_CHUNKS,)), dma, dma,
            dma((steps,)), dma((steps,)),
            dma((2, COL_PIECES)), dma((2, COL_PIECES)),
            dma((COL_PIECES,)), dma((COL_PIECES,)),
        ],
        compiler_params=pltpu.CompilerParams(
            collective_id=0, has_side_effects=True, vmem_limit_bytes=48 * 1024 * 1024
        ),
        name="rgcn",
    )(
        block_count, req_rows, req_slots, feats, rel_weight,
        bias.reshape(1, -1), gain.reshape(1, -1), offset.reshape(1, -1),
    )


def solution(mesh):
    return jax.shard_map(
        body,
        mesh=mesh,
        in_specs=(
            P(("dom", "row"), "feat"),
            P(("dom", "row"), None),
            P(("dom", "row"), None),
            P(("dom", "row"), None),
            P(None, "feat", None),
            P(),
            P(),
            P(),
        ),
        out_specs=P(("dom", "row", "feat"), None),
        check_vma=False,
    )
```

```python
import functools

import jax
import jax.numpy as jnp
from jax import lax
from jax.experimental import pallas as pl
from jax.experimental.pallas import tpu as pltpu
from jax.sharding import PartitionSpec as P

REL = 5
BLK = 128
MESH = pl.DeviceIdType.MESH
F32 = jnp.float32
BF16 = jnp.bfloat16

epsilon = 1e-05

FEAT_CHUNKS = 8
CAST_ROWS = 256
GATHER_UNROLL = 16
COL_PIECES = 4


def kernel(
    owners, bc_ref, rows_ref, slots_ref, feats_ref, weight_ref, bias_ref, gain_ref, offset_ref,
    out_ref,
    asked, feats_v, feats_f, weight_v, found, sent, got, block, agg, own_term, operand,
    part, half_in, half_out, last_in,
    asked_send, asked_recv, feats_sem, weight_sem, own_sem, row_send, row_recv,
    pair_send, pair_recv, far_send, far_recv,
):
    me = lax.axis_index("row")
    place = lax.axis_index("feat")
    high, low = place // 2, place % 2
    pair = {"feat": high * 2 + 1 - low}
    far = {"feat": (1 - high) * 2 + low}
    nodes, columns = feats_f.shape
    asks = slots_ref.shape[1] // owners
    half = asks // 2
    steps = owners - 1
    rows_out, width = out_ref.shape
    piece = width // COL_PIECES

    def shift(step):
        return 1 + lax.rem(owners // 2 - 1 + step, steps)

    def dest_of(step):
        return lax.rem(me + shift(step), owners)

    def owner_of(step):
        return lax.rem(me - shift(step) + owners, owners)

    def my_rows(owner):
        return rows_ref.at[:, pl.ds(pl.multiple_of(owner * asks, BLK), asks)]

    chunk_rows = nodes // FEAT_CHUNKS

    def feats_copy(c):
        span = pl.ds(pl.multiple_of(c * chunk_rows, chunk_rows), chunk_rows)
        return pltpu.make_async_copy(feats_ref.at[:, span], feats_v.at[:, span], feats_sem.at[c])

    for c in range(FEAT_CHUNKS):
        feats_copy(c).start()
    own_copy = pltpu.make_async_copy(my_rows(me), asked.at[steps], own_sem)
    own_copy.start()
    weight_copy = pltpu.make_async_copy(weight_ref, weight_v, weight_sem)
    weight_copy.start()

    barrier = pltpu.get_barrier_semaphore()

    @pl.loop(0, steps)
    def _(step):
        pl.semaphore_signal(barrier, inc=1, device_id={"row": dest_of(step)}, device_id_type=MESH)

    pl.semaphore_signal(barrier, inc=1, device_id=pair, device_id_type=MESH)
    pl.semaphore_signal(barrier, inc=1, device_id=far, device_id_type=MESH)
    pl.semaphore_wait(barrier, steps + 2)

    def ask(step):
        owner = owner_of(step)
        return pltpu.make_async_remote_copy(
            src_ref=my_rows(owner), dst_ref=asked.at[step],
            send_sem=asked_send.at[step], recv_sem=asked_recv.at[step],
            device_id={"row": owner}, device_id_type=MESH,
        )

    def answer(step):
        return pltpu.make_async_remote_copy(
            src_ref=sent.at[step], dst_ref=got.at[step],
            send_sem=row_send.at[step], recv_sem=row_recv.at[step],
            device_id={"row": dest_of(step)}, device_id_type=MESH,
        )

    @pl.loop(0, steps)
    def _(step):
        ask(step).start()

    unit_row = lax.broadcasted_iota(jnp.int32, (CAST_ROWS, CAST_ROWS), 0)
    unit_col = lax.broadcasted_iota(jnp.int32, (CAST_ROWS, CAST_ROWS), 1)
    unit = jnp.where(unit_row == unit_col, 1.0, 0.0).astype(BF16)

    @pl.loop(0, FEAT_CHUNKS)
    def _(c):
        feats_copy(c).wait()

        for i in range(chunk_rows // CAST_ROWS):
            span = pl.ds(pl.multiple_of(c * chunk_rows + i * CAST_ROWS, CAST_ROWS), CAST_ROWS)
            feats_f[span, :] = lax.dot_general(
                unit, feats_v[:, span], (((1,), (1,)), ((), ())), preferred_element_type=F32
            )

    def gather(step, put):
        @pl.loop(0, asks // GATHER_UNROLL)
        def _(g):
            base = pl.multiple_of(g * GATHER_UNROLL, GATHER_UNROLL)
            for u in range(GATHER_UNROLL):
                node = asked[step, 0, base + u]
                found[pl.ds(base + u, 1), :] = feats_f[pl.ds(node, 1), :]

        put(slice(0, asks), found[:, :BLK].astype(BF16))
        tail = columns - BLK
        first = found[pl.ds(0, half), BLK:columns]
        second = found[pl.ds(half, half), BLK:columns]
        put(slice(asks, asks + half), jnp.concatenate([first, second], axis=1).astype(BF16))

    @pl.loop(0, steps)
    def _(step):
        ask(step).wait_recv()

        def put(span, value):
            sent[step, span, :] = value

        gather(step, put)
        answer(step).start()

    own_copy.wait()

    def put_own(span, value):
        got[steps, span, :] = value

    gather(steps, put_own)

    weight_copy.wait()

    @pl.loop(0, 4)
    def _(c):
        span = pl.ds(pl.multiple_of(c * rows_out, rows_out), rows_out)
        own_term[c] = jnp.dot(feats_f[span, :].astype(BF16), weight_v[REL], preferred_element_type=F32)

    lane = lax.broadcasted_iota(jnp.int32, (asks, BLK), 1)

    def unpack(step):
        block[:, :BLK] = got[step, :asks, :]
        tails = got[step, asks:, :].astype(F32)
        both = jnp.concatenate([tails, pltpu.roll(tails, BLK // 2, 1)], axis=0)
        block[:, BLK:] = jnp.where(lane == columns - BLK, 1.0, both).astype(BF16)

    pos = lax.broadcasted_iota(jnp.int32, (1, asks), 1)

    def keys_of(owner):
        keys = slots_ref[:, pl.ds(pl.multiple_of(owner * asks, BLK), asks)]
        return jnp.where(pos < bc_ref[0, owner] * BLK, keys, -1)

    target = lax.broadcasted_iota(jnp.int32, (rows_out, asks), 0) * REL

    def sums(keys, chunk, rel):
        hits = target == keys - (chunk * rows_out * REL + rel)
        pick = jnp.where(hits, 1.0, 0.0).astype(BF16)
        return jnp.dot(pick, block[...], preferred_element_type=F32)

    unpack(steps)
    own_keys = keys_of(me)

    @pl.loop(0, 4)
    def _(chunk):
        for rel in range(REL):
            agg[chunk, rel] = sums(own_keys, chunk, rel)

    @pl.loop(0, steps - 1)
    def _(step):
        answer(step).wait_recv()
        unpack(step)
        keys = keys_of(owner_of(step))

        @pl.loop(0, 4)
        def _(chunk):
            for rel in range(REL):
                agg[chunk, rel] += sums(keys, chunk, rel)

    answer(steps - 1).wait_recv()
    unpack(steps - 1)
    last_keys = keys_of(owner_of(steps - 1))

    def operands(chunk):
        for rel in range(REL):
            total = agg[chunk, rel] + sums(last_keys, chunk, rel)
            count = total[:, columns:columns + 1]
            mean = total[:, :columns] * (1.0 / jnp.maximum(count, 1.0))
            operand[rel] = mean.astype(BF16)

    def project(chunk, q):
        cols = slice(q * piece, (q + 1) * piece)
        value = own_term[chunk, :, cols]
        for rel in range(REL):
            value += jnp.dot(operand[rel], weight_v[rel, :, cols], preferred_element_type=F32)
        return value

    def to_pair(i, q):
        return pltpu.make_async_remote_copy(
            src_ref=part.at[i, q], dst_ref=half_in.at[i, q],
            send_sem=pair_send.at[i, q], recv_sem=pair_recv.at[i, q],
            device_id=pair, device_id_type=MESH,
        )

    def to_far(q):
        return pltpu.make_async_remote_copy(
            src_ref=half_out.at[q], dst_ref=last_in.at[q],
            send_sem=far_send.at[q], recv_sem=far_recv.at[q],
            device_id=far, device_id_type=MESH,
        )

    chunk = (1 - high) * 2 + 1 - low
    operands(chunk)
    for q in range(COL_PIECES):
        part[0, q] = project(chunk, q)
        to_pair(0, q).start()

    chunk = (1 - high) * 2 + low
    operands(chunk)
    for q in range(COL_PIECES):
        value = project(chunk, q)
        to_pair(0, q).wait_recv()
        half_out[q] = value + half_in[0, q]
        to_far(q).start()

    chunk = high * 2 + 1 - low
    operands(chunk)
    for q in range(COL_PIECES):
        part[1, q] = project(chunk, q)
        to_pair(1, q).start()

    chunk = high * 2 + low
    operands(chunk)
    for q in range(COL_PIECES):
        cols = slice(q * piece, (q + 1) * piece)
        value = project(chunk, q)
        to_pair(1, q).wait_recv()
        own_term[chunk, :, cols] = value + half_in[1, q] + bias_ref[:, cols]

    total = jnp.zeros((rows_out, 1), F32)
    for q in range(COL_PIECES):
        cols = slice(q * piece, (q + 1) * piece)
        to_far(q).wait_recv()
        act = jnp.maximum(own_term[chunk, :, cols] + last_in[q], 0.0)
        last_in[q] = act
        total += jnp.sum(act, axis=1, keepdims=True)
    mu = total / width
    spread = jnp.zeros((rows_out, 1), F32)
    for q in range(COL_PIECES):
        dev = last_in[q] - mu
        spread += jnp.sum(dev * dev, axis=1, keepdims=True)
    scale = lax.rsqrt(spread / width + epsilon)
    for q in range(COL_PIECES):
        cols = slice(q * piece, (q + 1) * piece)
        dev = last_in[q] - mu
        out_ref[:, cols] = (dev * scale * gain_ref[:, cols] + offset_ref[:, cols]).astype(BF16)

    @pl.loop(0, steps)
    def _(step):
        ask(step).wait_send()
        answer(step).wait_send()

    for q in range(COL_PIECES):
        to_pair(0, q).wait_send()
        to_pair(1, q).wait_send()
        to_far(q).wait_send()


def body(feats, req_rows, req_slots, block_count, rel_weight, bias, gain, offset):
    owners = lax.axis_size("row")
    ranks = lax.axis_size("feat")
    nodes, columns = feats.shape
    rels, _, width = rel_weight.shape
    asks = req_rows.shape[1] // owners
    steps = owners - 1
    rows_out = 640 // ranks
    piece = width // COL_PIECES
    packed = asks + asks // 2
    dma = pltpu.SemaphoreType.DMA
    vmem = pl.BlockSpec(memory_space=pltpu.VMEM)
    hbm = pl.BlockSpec(memory_space=pl.ANY)
    return pl.pallas_call(
        functools.partial(kernel, owners),
        out_shape=jax.ShapeDtypeStruct((rows_out, width), BF16),
        in_specs=[pl.BlockSpec(memory_space=pltpu.SMEM), hbm, vmem, hbm, hbm, vmem, vmem, vmem],
        out_specs=vmem,
        scratch_shapes=[
            pltpu.SMEM((owners, 1, asks), jnp.int32),
            pltpu.VMEM((columns, nodes), BF16),
            pltpu.VMEM((nodes, columns), F32),
            pltpu.VMEM((rels, columns, width), BF16),
            pltpu.VMEM((asks, columns), F32),
            pltpu.VMEM((steps, packed, BLK), BF16),
            pltpu.VMEM((owners, packed, BLK), BF16),
            pltpu.VMEM((asks, 2 * BLK), BF16),
            pltpu.VMEM((ranks, REL, rows_out, 2 * BLK), F32),
            pltpu.VMEM((ranks, rows_out, width), F32),
            pltpu.VMEM((REL, rows_out, columns), BF16),
            pltpu.VMEM((2, COL_PIECES, rows_out, piece), F32),
            pltpu.VMEM((2, COL_PIECES, rows_out, piece), F32),
            pltpu.VMEM((COL_PIECES, rows_out, piece), F32),
            pltpu.VMEM((COL_PIECES, rows_out, piece), F32),
            dma((steps,)), dma((steps,)), dma((FEAT_CHUNKS,)), dma, dma,
            dma((steps,)), dma((steps,)),
            dma((2, COL_PIECES)), dma((2, COL_PIECES)),
            dma((COL_PIECES,)), dma((COL_PIECES,)),
        ],
        compiler_params=pltpu.CompilerParams(
            collective_id=0, has_side_effects=True, vmem_limit_bytes=60 * 1024 * 1024
        ),
        name="rgcn",
    )(
        block_count, req_rows, req_slots, feats.T, rel_weight,
        bias.reshape(1, -1), gain.reshape(1, -1), offset.reshape(1, -1),
    )


def solution(mesh):
    return jax.shard_map(
        body,
        mesh=mesh,
        in_specs=(
            P(("dom", "row"), "feat"),
            P(("dom", "row"), None),
            P(("dom", "row"), None),
            P(("dom", "row"), None),
            P(None, "feat", None),
            P(),
            P(),
            P(),
        ),
        out_specs=P(("dom", "row", "feat"), None),
        check_vma=False,
    )
```

```python
import functools

import jax
import jax.numpy as jnp
from jax import lax
from jax.experimental import pallas as pl
from jax.experimental.pallas import tpu as pltpu
from jax.sharding import PartitionSpec as P

REL = 5
BLK = 128
MESH = pl.DeviceIdType.MESH
F32 = jnp.float32
BF16 = jnp.bfloat16

epsilon = 1e-05

FEAT_CHUNKS = 8
CAST_ROWS = 256
GATHER_UNROLL = 16
COL_PIECES = 4
LEVELS = 32767.0
TINY = 1e-30


def kernel(
    owners, bc_ref, rows_ref, slots_ref, feats_ref, weight_ref, bias_ref, gain_ref, offset_ref,
    out_ref,
    asked, feats_v, feats_f, weight_v, found, sent, got, block, agg, own_term, operand,
    part, half_in, half_out, half_scale, last_in, last_scale, acted,
    asked_send, asked_recv, feats_sem, weight_sem, own_sem, row_send, row_recv,
    pair_send, pair_recv, far_send, far_recv, scale_send, scale_recv,
):
    me = lax.axis_index("row")
    place = lax.axis_index("feat")
    high, low = place // 2, place % 2
    pair = {"feat": high * 2 + 1 - low}
    far = {"feat": (1 - high) * 2 + low}
    nodes, columns = feats_f.shape
    asks = slots_ref.shape[1] // owners
    half = asks // 2
    steps = owners - 1
    rows_out, width = out_ref.shape
    piece = width // COL_PIECES

    def shift(step):
        return 1 + lax.rem(owners // 2 - 1 + step, steps)

    def dest_of(step):
        return lax.rem(me + shift(step), owners)

    def owner_of(step):
        return lax.rem(me - shift(step) + owners, owners)

    def my_rows(owner):
        return rows_ref.at[:, pl.ds(pl.multiple_of(owner * asks, BLK), asks)]

    chunk_rows = nodes // FEAT_CHUNKS

    def feats_copy(c):
        span = pl.ds(pl.multiple_of(c * chunk_rows, chunk_rows), chunk_rows)
        return pltpu.make_async_copy(feats_ref.at[:, span], feats_v.at[:, span], feats_sem.at[c])

    for c in range(FEAT_CHUNKS):
        feats_copy(c).start()
    own_copy = pltpu.make_async_copy(my_rows(me), asked.at[steps], own_sem)
    own_copy.start()
    weight_copy = pltpu.make_async_copy(weight_ref, weight_v, weight_sem)
    weight_copy.start()

    barrier = pltpu.get_barrier_semaphore()

    @pl.loop(0, steps)
    def _(step):
        pl.semaphore_signal(barrier, inc=1, device_id={"row": dest_of(step)}, device_id_type=MESH)

    pl.semaphore_signal(barrier, inc=1, device_id=pair, device_id_type=MESH)
    pl.semaphore_signal(barrier, inc=1, device_id=far, device_id_type=MESH)
    pl.semaphore_wait(barrier, steps + 2)

    def ask(step):
        owner = owner_of(step)
        return pltpu.make_async_remote_copy(
            src_ref=my_rows(owner), dst_ref=asked.at[step],
            send_sem=asked_send.at[step], recv_sem=asked_recv.at[step],
            device_id={"row": owner}, device_id_type=MESH,
        )

    def answer(step):
        return pltpu.make_async_remote_copy(
            src_ref=sent.at[step], dst_ref=got.at[step],
            send_sem=row_send.at[step], recv_sem=row_recv.at[step],
            device_id={"row": dest_of(step)}, device_id_type=MESH,
        )

    @pl.loop(0, steps)
    def _(step):
        ask(step).start()

    unit_row = lax.broadcasted_iota(jnp.int32, (CAST_ROWS, CAST_ROWS), 0)
    unit_col = lax.broadcasted_iota(jnp.int32, (CAST_ROWS, CAST_ROWS), 1)
    unit = jnp.where(unit_row == unit_col, 1.0, 0.0).astype(BF16)

    @pl.loop(0, FEAT_CHUNKS)
    def _(c):
        feats_copy(c).wait()

        for i in range(chunk_rows // CAST_ROWS):
            span = pl.ds(pl.multiple_of(c * chunk_rows + i * CAST_ROWS, CAST_ROWS), CAST_ROWS)
            feats_f[span, :] = lax.dot_general(
                unit, feats_v[:, span], (((1,), (1,)), ((), ())), preferred_element_type=F32
            )

    def gather(step, put):
        @pl.loop(0, asks // GATHER_UNROLL)
        def _(g):
            base = pl.multiple_of(g * GATHER_UNROLL, GATHER_UNROLL)
            for u in range(GATHER_UNROLL):
                node = asked[step, 0, base + u]
                found[pl.ds(base + u, 1), :] = feats_f[pl.ds(node, 1), :]

        put(slice(0, asks), found[:, :BLK].astype(BF16))
        tail = columns - BLK
        first = found[pl.ds(0, half), BLK:columns]
        second = found[pl.ds(half, half), BLK:columns]
        put(slice(asks, asks + half), jnp.concatenate([first, second], axis=1).astype(BF16))

    @pl.loop(0, steps)
    def _(step):
        ask(step).wait_recv()

        def put(span, value):
            sent[step, span, :] = value

        gather(step, put)
        answer(step).start()

    own_copy.wait()

    def put_own(span, value):
        got[steps, span, :] = value

    gather(steps, put_own)

    weight_copy.wait()

    @pl.loop(0, 4)
    def _(c):
        span = pl.ds(pl.multiple_of(c * rows_out, rows_out), rows_out)
        own_term[c] = jnp.dot(feats_f[span, :].astype(BF16), weight_v[REL], preferred_element_type=F32)

    lane = lax.broadcasted_iota(jnp.int32, (asks, BLK), 1)

    def unpack(step):
        block[:, :BLK] = got[step, :asks, :]
        tails = got[step, asks:, :].astype(F32)
        both = jnp.concatenate([tails, pltpu.roll(tails, BLK // 2, 1)], axis=0)
        block[:, BLK:] = jnp.where(lane == columns - BLK, 1.0, both).astype(BF16)

    pos = lax.broadcasted_iota(jnp.int32, (1, asks), 1)

    def keys_of(owner):
        keys = slots_ref[:, pl.ds(pl.multiple_of(owner * asks, BLK), asks)]
        return jnp.where(pos < bc_ref[0, owner] * BLK, keys, -1)

    target = lax.broadcasted_iota(jnp.int32, (rows_out, asks), 0) * REL

    def sums(keys, chunk, rel):
        hits = target == keys - (chunk * rows_out * REL + rel)
        pick = jnp.where(hits, 1.0, 0.0).astype(BF16)
        return jnp.dot(pick, block[...], preferred_element_type=F32)

    unpack(steps)
    own_keys = keys_of(me)

    @pl.loop(0, 4)
    def _(chunk):
        for rel in range(REL):
            agg[chunk, rel] = sums(own_keys, chunk, rel)

    @pl.loop(0, steps - 1)
    def _(step):
        answer(step).wait_recv()
        unpack(step)
        keys = keys_of(owner_of(step))

        @pl.loop(0, 4)
        def _(chunk):
            for rel in range(REL):
                agg[chunk, rel] += sums(keys, chunk, rel)

    answer(steps - 1).wait_recv()
    unpack(steps - 1)
    last_keys = keys_of(owner_of(steps - 1))

    def operands(chunk):
        for rel in range(REL):
            total = agg[chunk, rel] + sums(last_keys, chunk, rel)
            count = total[:, columns:columns + 1]
            mean = total[:, :columns] * (1.0 / jnp.maximum(count, 1.0))
            operand[rel] = mean.astype(BF16)

    def project(chunk, q):
        cols = slice(q * piece, (q + 1) * piece)
        value = own_term[chunk, :, cols]
        for rel in range(REL):
            value += jnp.dot(operand[rel], weight_v[rel, :, cols], preferred_element_type=F32)
        return value

    def to_pair(i, q):
        return pltpu.make_async_remote_copy(
            src_ref=part.at[i, q], dst_ref=half_in.at[i, q],
            send_sem=pair_send.at[i, q], recv_sem=pair_recv.at[i, q],
            device_id=pair, device_id_type=MESH,
        )

    def to_far(q):
        return pltpu.make_async_remote_copy(
            src_ref=half_out.at[q], dst_ref=last_in.at[q],
            send_sem=far_send.at[q], recv_sem=far_recv.at[q],
            device_id=far, device_id_type=MESH,
        )

    def scale_to_far(q):
        return pltpu.make_async_remote_copy(
            src_ref=half_scale.at[q], dst_ref=last_scale.at[q],
            send_sem=scale_send.at[q], recv_sem=scale_recv.at[q],
            device_id=far, device_id_type=MESH,
        )

    def encode(q, value):
        top = jnp.maximum(jnp.max(jnp.abs(value), axis=1, keepdims=True), TINY)
        step = jnp.broadcast_to(top * (1.0 / LEVELS), (rows_out, BLK))
        half_scale[q] = jnp.transpose(step)[:1, :]
        half_out[q] = jnp.round(value * (LEVELS / top)).astype(jnp.int32).astype(jnp.int16)

    def decode(q):
        step = jnp.transpose(jnp.broadcast_to(last_scale[q], (BLK, rows_out)))
        step = jnp.concatenate([step] * (piece // BLK), axis=1)
        return last_in[q].astype(jnp.int32).astype(F32) * step

    chunk = (1 - high) * 2 + 1 - low
    operands(chunk)
    for q in range(COL_PIECES):
        part[0, q] = project(chunk, q)
        to_pair(0, q).start()

    chunk = (1 - high) * 2 + low
    operands(chunk)
    for q in range(COL_PIECES):
        value = project(chunk, q)
        to_pair(0, q).wait_recv()
        encode(q, value + half_in[0, q])
        scale_to_far(q).start()
        to_far(q).start()

    chunk = high * 2 + 1 - low
    operands(chunk)
    for q in range(COL_PIECES):
        part[1, q] = project(chunk, q)
        to_pair(1, q).start()

    chunk = high * 2 + low
    operands(chunk)
    for q in range(COL_PIECES):
        cols = slice(q * piece, (q + 1) * piece)
        value = project(chunk, q)
        to_pair(1, q).wait_recv()
        own_term[chunk, :, cols] = value + half_in[1, q] + bias_ref[:, cols]

    total = jnp.zeros((rows_out, 1), F32)
    for q in range(COL_PIECES):
        cols = slice(q * piece, (q + 1) * piece)
        scale_to_far(q).wait_recv()
        to_far(q).wait_recv()
        act = jnp.maximum(own_term[chunk, :, cols] + decode(q), 0.0)
        acted[q] = act
        total += jnp.sum(act, axis=1, keepdims=True)
    mu = total / width
    spread = jnp.zeros((rows_out, 1), F32)
    for q in range(COL_PIECES):
        dev = acted[q] - mu
        spread += jnp.sum(dev * dev, axis=1, keepdims=True)
    scale = lax.rsqrt(spread / width + epsilon)
    for q in range(COL_PIECES):
        cols = slice(q * piece, (q + 1) * piece)
        dev = acted[q] - mu
        out_ref[:, cols] = (dev * scale * gain_ref[:, cols] + offset_ref[:, cols]).astype(BF16)

    @pl.loop(0, steps)
    def _(step):
        ask(step).wait_send()
        answer(step).wait_send()

    for q in range(COL_PIECES):
        to_pair(0, q).wait_send()
        to_pair(1, q).wait_send()
        scale_to_far(q).wait_send()
        to_far(q).wait_send()


def body(feats, req_rows, req_slots, block_count, rel_weight, bias, gain, offset):
    owners = lax.axis_size("row")
    ranks = lax.axis_size("feat")
    nodes, columns = feats.shape
    rels, _, width = rel_weight.shape
    asks = req_rows.shape[1] // owners
    steps = owners - 1
    rows_out = 640 // ranks
    piece = width // COL_PIECES
    packed = asks + asks // 2
    dma = pltpu.SemaphoreType.DMA
    vmem = pl.BlockSpec(memory_space=pltpu.VMEM)
    hbm = pl.BlockSpec(memory_space=pl.ANY)
    return pl.pallas_call(
        functools.partial(kernel, owners),
        out_shape=jax.ShapeDtypeStruct((rows_out, width), BF16),
        in_specs=[pl.BlockSpec(memory_space=pltpu.SMEM), hbm, vmem, hbm, hbm, vmem, vmem, vmem],
        out_specs=vmem,
        scratch_shapes=[
            pltpu.SMEM((owners, 1, asks), jnp.int32),
            pltpu.VMEM((columns, nodes), BF16),
            pltpu.VMEM((nodes, columns), F32),
            pltpu.VMEM((rels, columns, width), BF16),
            pltpu.VMEM((asks, columns), F32),
            pltpu.VMEM((steps, packed, BLK), BF16),
            pltpu.VMEM((owners, packed, BLK), BF16),
            pltpu.VMEM((asks, 2 * BLK), BF16),
            pltpu.VMEM((ranks, REL, rows_out, 2 * BLK), F32),
            pltpu.VMEM((ranks, rows_out, width), F32),
            pltpu.VMEM((REL, rows_out, columns), BF16),
            pltpu.VMEM((2, COL_PIECES, rows_out, piece), F32),
            pltpu.VMEM((2, COL_PIECES, rows_out, piece), F32),
            pltpu.VMEM((COL_PIECES, rows_out, piece), jnp.int16),
            pltpu.VMEM((COL_PIECES, 1, rows_out), F32),
            pltpu.VMEM((COL_PIECES, rows_out, piece), jnp.int16),
            pltpu.VMEM((COL_PIECES, 1, rows_out), F32),
            pltpu.VMEM((COL_PIECES, rows_out, piece), F32),
            dma((steps,)), dma((steps,)), dma((FEAT_CHUNKS,)), dma, dma,
            dma((steps,)), dma((steps,)),
            dma((2, COL_PIECES)), dma((2, COL_PIECES)),
            dma((COL_PIECES,)), dma((COL_PIECES,)), dma((COL_PIECES,)), dma((COL_PIECES,)),
        ],
        compiler_params=pltpu.CompilerParams(
            collective_id=0, has_side_effects=True, vmem_limit_bytes=60 * 1024 * 1024
        ),
        name="rgcn",
    )(
        block_count, req_rows, req_slots, feats.T, rel_weight,
        bias.reshape(1, -1), gain.reshape(1, -1), offset.reshape(1, -1),
    )


def solution(mesh):
    return jax.shard_map(
        body,
        mesh=mesh,
        in_specs=(
            P(("dom", "row"), "feat"),
            P(("dom", "row"), None),
            P(("dom", "row"), None),
            P(("dom", "row"), None),
            P(None, "feat", None),
            P(),
            P(),
            P(),
        ),
        out_specs=P(("dom", "row", "feat"), None),
        check_vma=False,
    )
```

```python
import functools

import jax
import jax.numpy as jnp
from jax import lax
from jax.experimental import pallas as pl
from jax.experimental.pallas import tpu as pltpu
from jax.sharding import PartitionSpec as P

REL = 5
BLK = 128
MESH = pl.DeviceIdType.MESH
F32 = jnp.float32
BF16 = jnp.bfloat16

epsilon = 1e-05

FEAT_CHUNKS = 8
CAST_ROWS = 256
GATHER_UNROLL = 16
COL_PIECES = 4
SHARES = 2
LEVELS = 32767.0
TINY = 1e-30


def kernel(
    owners, bc_ref, rows_ref, slots_ref, feats_ref, weight_ref, bias_ref, gain_ref, offset_ref,
    out_ref,
    asked, feats_v, feats_f, weight_v, found, sent, got, block, agg, own_term, operand,
    part, half_in, half_out, half_scale, last_in, last_scale, acted,
    asked_send, asked_recv, feats_sem, weight_sem, own_sem, row_send, row_recv,
    pair_send, pair_recv, far_send, far_recv, scale_send, scale_recv,
):
    me = lax.axis_index("row")
    place = lax.axis_index("feat")
    high, low = place // 2, place % 2
    pair = {"feat": high * 2 + 1 - low}
    far = {"feat": (1 - high) * 2 + low}
    nodes, columns = feats_f.shape
    asks = slots_ref.shape[1] // owners
    share = asks // SHARES
    half = share // 2
    steps = owners - 1
    rows_out, width = out_ref.shape
    piece = width // COL_PIECES

    def shift(step):
        return 1 + lax.rem(owners // 2 - 1 + step, steps)

    def dest_of(step):
        return lax.rem(me + shift(step), owners)

    def owner_of(step):
        return lax.rem(me - shift(step) + owners, owners)

    def my_rows(owner):
        return rows_ref.at[:, pl.ds(pl.multiple_of(owner * asks, BLK), asks)]

    chunk_rows = nodes // FEAT_CHUNKS

    def feats_copy(c):
        span = pl.ds(pl.multiple_of(c * chunk_rows, chunk_rows), chunk_rows)
        return pltpu.make_async_copy(feats_ref.at[:, span], feats_v.at[:, span], feats_sem.at[c])

    for c in range(FEAT_CHUNKS):
        feats_copy(c).start()
    own_copy = pltpu.make_async_copy(my_rows(me), asked.at[steps], own_sem)
    own_copy.start()
    weight_copy = pltpu.make_async_copy(weight_ref, weight_v, weight_sem)
    weight_copy.start()

    barrier = pltpu.get_barrier_semaphore()

    @pl.loop(0, steps)
    def _(step):
        pl.semaphore_signal(barrier, inc=1, device_id={"row": dest_of(step)}, device_id_type=MESH)

    pl.semaphore_signal(barrier, inc=1, device_id=pair, device_id_type=MESH)
    pl.semaphore_signal(barrier, inc=1, device_id=far, device_id_type=MESH)
    pl.semaphore_wait(barrier, steps + 2)

    def ask(step):
        owner = owner_of(step)
        return pltpu.make_async_remote_copy(
            src_ref=my_rows(owner), dst_ref=asked.at[step],
            send_sem=asked_send.at[step], recv_sem=asked_recv.at[step],
            device_id={"row": owner}, device_id_type=MESH,
        )

    def answer(step, k):
        return pltpu.make_async_remote_copy(
            src_ref=sent.at[step, k], dst_ref=got.at[step, k],
            send_sem=row_send.at[step, k], recv_sem=row_recv.at[step, k],
            device_id={"row": dest_of(step)}, device_id_type=MESH,
        )

    @pl.loop(0, steps)
    def _(step):
        ask(step).start()

    unit_row = lax.broadcasted_iota(jnp.int32, (CAST_ROWS, CAST_ROWS), 0)
    unit_col = lax.broadcasted_iota(jnp.int32, (CAST_ROWS, CAST_ROWS), 1)
    unit = jnp.where(unit_row == unit_col, 1.0, 0.0).astype(BF16)

    @pl.loop(0, FEAT_CHUNKS)
    def _(c):
        feats_copy(c).wait()

        for i in range(chunk_rows // CAST_ROWS):
            span = pl.ds(pl.multiple_of(c * chunk_rows + i * CAST_ROWS, CAST_ROWS), CAST_ROWS)
            feats_f[span, :] = lax.dot_general(
                unit, feats_v[:, span], (((1,), (1,)), ((), ())), preferred_element_type=F32
            )

    def gather(step, k, to):
        @pl.loop(0, share // GATHER_UNROLL)
        def _(g):
            base = pl.multiple_of(g * GATHER_UNROLL, GATHER_UNROLL)
            for u in range(GATHER_UNROLL):
                node = asked[step, 0, k * share + base + u]
                found[pl.ds(base + u, 1), :] = feats_f[pl.ds(node, 1), :]

        to[step, k, :share, :] = found[:, :BLK].astype(BF16)
        first = found[:half, BLK:]
        second = found[half:, BLK:]
        to[step, k, share:, :] = jnp.concatenate([first, second], axis=1).astype(BF16)

    @pl.loop(0, steps)
    def _(step):
        ask(step).wait_recv()
        for k in range(SHARES):
            gather(step, k, sent)
            answer(step, k).start()

    own_copy.wait()
    for k in range(SHARES):
        gather(steps, k, got)

    weight_copy.wait()

    @pl.loop(0, 4)
    def _(c):
        span = pl.ds(pl.multiple_of(c * rows_out, rows_out), rows_out)
        own_term[c] = jnp.dot(feats_f[span, :].astype(BF16), weight_v[REL], preferred_element_type=F32)

    lane = lax.broadcasted_iota(jnp.int32, (share, BLK), 1)

    def unpack(step, at):
        for k in range(SHARES):
            span = slice(at + k * share, at + (k + 1) * share)
            block[span, :BLK] = got[step, k, :share, :]
            tails = got[step, k, share:, :].astype(F32)
            both = jnp.concatenate([tails, pltpu.roll(tails, BLK // 2, 1)], axis=0)
            block[span, BLK:] = jnp.where(lane == columns - BLK, 1.0, both).astype(BF16)

    pos = lax.broadcasted_iota(jnp.int32, (1, asks), 1)

    def keys_of(owner):
        keys = slots_ref[:, pl.ds(pl.multiple_of(owner * asks, BLK), asks)]
        return jnp.where(pos < bc_ref[0, owner] * BLK, keys, -1)

    def sums(keys, chunk, rel):
        depth = keys.shape[1]
        target = lax.broadcasted_iota(jnp.int32, (rows_out, depth), 0) * REL
        hits = target == keys - (chunk * rows_out * REL + rel)
        pick = jnp.where(hits, 1.0, 0.0).astype(BF16)
        return jnp.dot(pick, block[:depth, :], preferred_element_type=F32)

    unpack(steps, 0)
    own_keys = keys_of(me)

    @pl.loop(0, 4)
    def _(chunk):
        for rel in range(REL):
            agg[chunk, rel] = sums(own_keys, chunk, rel)

    @pl.loop(0, steps - 2)
    def _(step):
        for k in range(SHARES):
            answer(step, k).wait_recv()
        unpack(step, 0)
        keys = keys_of(owner_of(step))

        @pl.loop(0, 4)
        def _(chunk):
            for rel in range(REL):
                agg[chunk, rel] += sums(keys, chunk, rel)

    for i in range(2):
        for k in range(SHARES):
            answer(steps - 2 + i, k).wait_recv()
        unpack(steps - 2 + i, i * asks)
    last_keys = jnp.concatenate([keys_of(owner_of(steps - 2)), keys_of(owner_of(steps - 1))], axis=1)

    def operands(chunk):
        for rel in range(REL):
            total = agg[chunk, rel] + sums(last_keys, chunk, rel)
            count = total[:, columns:columns + 1]
            mean = total[:, :columns] * (1.0 / jnp.maximum(count, 1.0))
            operand[rel] = mean.astype(BF16)

    def project(chunk, q):
        cols = slice(q * piece, (q + 1) * piece)
        value = own_term[chunk, :, cols]
        for rel in range(REL):
            value += jnp.dot(operand[rel], weight_v[rel, :, cols], preferred_element_type=F32)
        return value

    def to_pair(i, q):
        return pltpu.make_async_remote_copy(
            src_ref=part.at[i, q], dst_ref=half_in.at[i, q],
            send_sem=pair_send.at[i, q], recv_sem=pair_recv.at[i, q],
            device_id=pair, device_id_type=MESH,
        )

    def to_far(q):
        return pltpu.make_async_remote_copy(
            src_ref=half_out.at[q], dst_ref=last_in.at[q],
            send_sem=far_send.at[q], recv_sem=far_recv.at[q],
            device_id=far, device_id_type=MESH,
        )

    def scale_to_far(q):
        return pltpu.make_async_remote_copy(
            src_ref=half_scale.at[q], dst_ref=last_scale.at[q],
            send_sem=scale_send.at[q], recv_sem=scale_recv.at[q],
            device_id=far, device_id_type=MESH,
        )

    def encode(q, value):
        top = jnp.maximum(jnp.max(jnp.abs(value), axis=1, keepdims=True), TINY)
        step = jnp.broadcast_to(top * (1.0 / LEVELS), (rows_out, BLK))
        half_scale[q] = jnp.transpose(step)[:1, :]
        half_out[q] = jnp.round(value * (LEVELS / top)).astype(jnp.int32).astype(jnp.int16)

    def decode(q):
        step = jnp.transpose(jnp.broadcast_to(last_scale[q], (BLK, rows_out)))
        step = jnp.concatenate([step] * (piece // BLK), axis=1)
        return last_in[q].astype(jnp.int32).astype(F32) * step

    chunk = (1 - high) * 2 + 1 - low
    operands(chunk)
    for q in range(COL_PIECES):
        part[0, q] = project(chunk, q)
        to_pair(0, q).start()

    chunk = (1 - high) * 2 + low
    operands(chunk)
    for q in range(COL_PIECES):
        value = project(chunk, q)
        to_pair(0, q).wait_recv()
        encode(q, value + half_in[0, q])
        scale_to_far(q).start()
        to_far(q).start()

    chunk = high * 2 + 1 - low
    operands(chunk)
    for q in range(COL_PIECES):
        part[1, q] = project(chunk, q)
        to_pair(1, q).start()

    chunk = high * 2 + low
    operands(chunk)
    for q in range(COL_PIECES):
        cols = slice(q * piece, (q + 1) * piece)
        value = project(chunk, q)
        to_pair(1, q).wait_recv()
        own_term[chunk, :, cols] = value + half_in[1, q] + bias_ref[:, cols]

    total = jnp.zeros((rows_out, 1), F32)
    for q in range(COL_PIECES):
        cols = slice(q * piece, (q + 1) * piece)
        scale_to_far(q).wait_recv()
        to_far(q).wait_recv()
        act = jnp.maximum(own_term[chunk, :, cols] + decode(q), 0.0)
        acted[q] = act
        total += jnp.sum(act, axis=1, keepdims=True)
    mu = total / width
    spread = jnp.zeros((rows_out, 1), F32)
    for q in range(COL_PIECES):
        dev = acted[q] - mu
        spread += jnp.sum(dev * dev, axis=1, keepdims=True)
    scale = lax.rsqrt(spread / width + epsilon)
    for q in range(COL_PIECES):
        cols = slice(q * piece, (q + 1) * piece)
        dev = acted[q] - mu
        out_ref[:, cols] = (dev * scale * gain_ref[:, cols] + offset_ref[:, cols]).astype(BF16)

    @pl.loop(0, steps)
    def _(step):
        ask(step).wait_send()
        for k in range(SHARES):
            answer(step, k).wait_send()

    for q in range(COL_PIECES):
        to_pair(0, q).wait_send()
        to_pair(1, q).wait_send()
        scale_to_far(q).wait_send()
        to_far(q).wait_send()


def body(feats, req_rows, req_slots, block_count, rel_weight, bias, gain, offset):
    owners = lax.axis_size("row")
    ranks = lax.axis_size("feat")
    nodes, columns = feats.shape
    rels, _, width = rel_weight.shape
    asks = req_rows.shape[1] // owners
    steps = owners - 1
    rows_out = 640 // ranks
    piece = width // COL_PIECES
    share = asks // SHARES
    packed = share + share // 2
    dma = pltpu.SemaphoreType.DMA
    vmem = pl.BlockSpec(memory_space=pltpu.VMEM)
    hbm = pl.BlockSpec(memory_space=pl.ANY)
    return pl.pallas_call(
        functools.partial(kernel, owners),
        out_shape=jax.ShapeDtypeStruct((rows_out, width), BF16),
        in_specs=[pl.BlockSpec(memory_space=pltpu.SMEM), hbm, vmem, hbm, hbm, vmem, vmem, vmem],
        out_specs=vmem,
        scratch_shapes=[
            pltpu.SMEM((owners, 1, asks), jnp.int32),
            pltpu.VMEM((columns, nodes), BF16),
            pltpu.VMEM((nodes, columns), F32),
            pltpu.VMEM((rels, columns, width), BF16),
            pltpu.VMEM((share, columns), F32),
            pltpu.VMEM((steps, SHARES, packed, BLK), BF16),
            pltpu.VMEM((owners, SHARES, packed, BLK), BF16),
            pltpu.VMEM((2 * asks, 2 * BLK), BF16),
            pltpu.VMEM((ranks, REL, rows_out, 2 * BLK), F32),
            pltpu.VMEM((ranks, rows_out, width), F32),
            pltpu.VMEM((REL, rows_out, columns), BF16),
            pltpu.VMEM((2, COL_PIECES, rows_out, piece), F32),
            pltpu.VMEM((2, COL_PIECES, rows_out, piece), F32),
            pltpu.VMEM((COL_PIECES, rows_out, piece), jnp.int16),
            pltpu.VMEM((COL_PIECES, 1, rows_out), F32),
            pltpu.VMEM((COL_PIECES, rows_out, piece), jnp.int16),
            pltpu.VMEM((COL_PIECES, 1, rows_out), F32),
            pltpu.VMEM((COL_PIECES, rows_out, piece), F32),
            dma((steps,)), dma((steps,)), dma((FEAT_CHUNKS,)), dma, dma,
            dma((steps, SHARES)), dma((steps, SHARES)),
            dma((2, COL_PIECES)), dma((2, COL_PIECES)),
            dma((COL_PIECES,)), dma((COL_PIECES,)), dma((COL_PIECES,)), dma((COL_PIECES,)),
        ],
        compiler_params=pltpu.CompilerParams(
            collective_id=0, has_side_effects=True, vmem_limit_bytes=60 * 1024 * 1024
        ),
        name="rgcn",
    )(
        block_count, req_rows, req_slots, feats.T, rel_weight,
        bias.reshape(1, -1), gain.reshape(1, -1), offset.reshape(1, -1),
    )


def solution(mesh):
    return jax.shard_map(
        body,
        mesh=mesh,
        in_specs=(
            P(("dom", "row"), "feat"),
            P(("dom", "row"), None),
            P(("dom", "row"), None),
            P(("dom", "row"), None),
            P(None, "feat", None),
            P(),
            P(),
            P(),
        ),
        out_specs=P(("dom", "row", "feat"), None),
        check_vma=False,
    )
```

```python
import functools

import jax
import jax.numpy as jnp
from jax import lax
from jax.experimental import pallas as pl
from jax.experimental.pallas import tpu as pltpu
from jax.sharding import PartitionSpec as P

REL = 5
BLK = 128
MESH = pl.DeviceIdType.MESH
F32 = jnp.float32
BF16 = jnp.bfloat16

epsilon = 1e-05

FEAT_CHUNKS = 8
CAST_ROWS = 256
GATHER_UNROLL = 16
COL_PIECES = 4
SHARES = 3
LEVELS = 32767.0
TINY = 1e-30


def kernel(
    owners, bc_hbm, rows_ref, slots_hbm, feats_ref, weight_ref, bias_hbm, gain_hbm, offset_hbm,
    out_ref,
    bc_ref, slots_ref, bias_ref, gain_ref, offset_ref, small_sem,
    asked, feats_v, feats_f, weight_v, found, sent, got, block, agg, own_term, operand,
    part, half_in, half_out, half_scale, last_in, last_scale, acted,
    asked_send, asked_recv, feats_sem, weight_sem, own_sem, row_send, row_recv,
    pair_send, pair_recv, far_send, far_recv, scale_send, scale_recv,
):
    me = lax.axis_index("row")
    place = lax.axis_index("feat")
    high, low = place // 2, place % 2
    pair = {"feat": high * 2 + 1 - low}
    far = {"feat": (1 - high) * 2 + low}
    nodes, columns = feats_f.shape
    asks = rows_ref.shape[1] // owners
    share = asks // SHARES
    half = share // 2
    steps = owners - 1
    rows_out, width = out_ref.shape
    piece = width // COL_PIECES

    def shift(step):
        return 1 + lax.rem(owners // 2 - 1 + step, steps)

    def dest_of(step):
        return lax.rem(me + shift(step), owners)

    def owner_of(step):
        return lax.rem(me - shift(step) + owners, owners)

    def my_rows(owner):
        return rows_ref.at[:, pl.ds(pl.multiple_of(owner * asks, BLK), asks)]

    barrier = pltpu.get_barrier_semaphore()

    @pl.loop(0, steps)
    def _(step):
        pl.semaphore_signal(barrier, inc=1, device_id={"row": dest_of(step)}, device_id_type=MESH)

    pl.semaphore_signal(barrier, inc=1, device_id=pair, device_id_type=MESH)
    pl.semaphore_signal(barrier, inc=1, device_id=far, device_id_type=MESH)
    chunk_rows = nodes // FEAT_CHUNKS

    def feats_copy(c):
        span = pl.ds(pl.multiple_of(c * chunk_rows, chunk_rows), chunk_rows)
        return pltpu.make_async_copy(feats_ref.at[:, span], feats_v.at[:, span], feats_sem.at[c])

    for c in range(FEAT_CHUNKS):
        feats_copy(c).start()
    own_copy = pltpu.make_async_copy(my_rows(me), asked.at[steps], own_sem)
    own_copy.start()
    weight_copy = pltpu.make_async_copy(weight_ref, weight_v, weight_sem)
    weight_copy.start()
    small = [
        pltpu.make_async_copy(src, dst, small_sem.at[i])
        for i, (src, dst) in enumerate([
            (bc_hbm, bc_ref), (slots_hbm, slots_ref), (bias_hbm, bias_ref),
            (gain_hbm, gain_ref), (offset_hbm, offset_ref),
        ])
    ]
    for copy in small:
        copy.start()

    def ask(step):
        owner = owner_of(step)
        return pltpu.make_async_remote_copy(
            src_ref=my_rows(owner), dst_ref=asked.at[step],
            send_sem=asked_send.at[step], recv_sem=asked_recv.at[step],
            device_id={"row": owner}, device_id_type=MESH,
        )

    def answer(step, k):
        return pltpu.make_async_remote_copy(
            src_ref=sent.at[step, k], dst_ref=got.at[step, k],
            send_sem=row_send.at[step, k], recv_sem=row_recv.at[step, k],
            device_id={"row": dest_of(step)}, device_id_type=MESH,
        )

    unit_row = lax.broadcasted_iota(jnp.int32, (CAST_ROWS, CAST_ROWS), 0)
    unit_col = lax.broadcasted_iota(jnp.int32, (CAST_ROWS, CAST_ROWS), 1)
    unit = jnp.where(unit_row == unit_col, 1.0, 0.0).astype(BF16)

    def turn(c):
        feats_copy(c).wait()

        for i in range(chunk_rows // CAST_ROWS):
            span = pl.ds(pl.multiple_of(c * chunk_rows + i * CAST_ROWS, CAST_ROWS), CAST_ROWS)
            feats_f[span, :] = lax.dot_general(
                unit, feats_v[:, span], (((1,), (1,)), ((), ())), preferred_element_type=F32
            )

    pl.loop(0, FEAT_CHUNKS // 2)(turn)
    pl.semaphore_wait(barrier, steps + 2)

    @pl.loop(0, steps)
    def _(step):
        ask(step).start()

    pl.loop(FEAT_CHUNKS // 2, FEAT_CHUNKS)(turn)

    def gather(step, k, to):
        @pl.loop(0, share // GATHER_UNROLL)
        def _(g):
            base = pl.multiple_of(g * GATHER_UNROLL, GATHER_UNROLL)
            for u in range(GATHER_UNROLL):
                node = asked[step, 0, k * share + base + u]
                found[pl.ds(base + u, 1), :] = feats_f[pl.ds(node, 1), :]

        to[step, k, :share, :] = found[:, :BLK].astype(BF16)
        first = found[:half, BLK:]
        second = found[half:, BLK:]
        to[step, k, share:, :] = jnp.concatenate([first, second], axis=1).astype(BF16)

    own_copy.wait()
    for k in range(SHARES):
        gather(steps, k, got)

    @pl.loop(0, steps)
    def _(step):
        ask(step).wait_recv()
        for k in range(SHARES):
            gather(step, k, sent)
            answer(step, k).start()

    weight_copy.wait()
    for copy in small:
        copy.wait()

    @pl.loop(0, 4)
    def _(c):
        span = pl.ds(pl.multiple_of(c * rows_out, rows_out), rows_out)
        own_term[c] = jnp.dot(feats_f[span, :].astype(BF16), weight_v[REL], preferred_element_type=F32)

    lane = lax.broadcasted_iota(jnp.int32, (share, BLK), 1)

    def unpack(step, at):
        for k in range(SHARES):
            span = slice(at + k * share, at + (k + 1) * share)
            block[span, :BLK] = got[step, k, :share, :]
            tails = got[step, k, share:, :].astype(F32)
            both = jnp.concatenate([tails, pltpu.roll(tails, BLK // 2, 1)], axis=0)
            block[span, BLK:] = jnp.where(lane == columns - BLK, 1.0, both).astype(BF16)

    pos = lax.broadcasted_iota(jnp.int32, (1, asks), 1)

    def keys_of(owner):
        keys = slots_ref[:, pl.ds(pl.multiple_of(owner * asks, BLK), asks)]
        return jnp.where(pos < bc_ref[0, owner] * BLK, keys, -1)

    def sums(keys, chunk, rel):
        depth = keys.shape[1]
        target = lax.broadcasted_iota(jnp.int32, (rows_out, depth), 0) * REL
        hits = target == keys - (chunk * rows_out * REL + rel)
        pick = jnp.where(hits, 1.0, 0.0).astype(BF16)
        return jnp.dot(pick, block[:depth, :], preferred_element_type=F32)

    unpack(steps, 0)
    own_keys = keys_of(me)

    @pl.loop(0, 4)
    def _(chunk):
        for rel in range(REL):
            agg[chunk, rel] = sums(own_keys, chunk, rel)

    @pl.loop(0, steps - 2)
    def _(step):
        for k in range(SHARES):
            answer(step, k).wait_recv()
        unpack(step, 0)
        keys = keys_of(owner_of(step))

        @pl.loop(0, 4)
        def _(chunk):
            for rel in range(REL):
                agg[chunk, rel] += sums(keys, chunk, rel)

    for i in range(2):
        for k in range(SHARES):
            answer(steps - 2 + i, k).wait_recv()
        unpack(steps - 2 + i, i * asks)
    last_keys = jnp.concatenate([keys_of(owner_of(steps - 2)), keys_of(owner_of(steps - 1))], axis=1)

    def operands(chunk):
        for rel in range(REL):
            total = agg[chunk, rel] + sums(last_keys, chunk, rel)
            count = total[:, columns:columns + 1]
            mean = total[:, :columns] * (1.0 / jnp.maximum(count, 1.0))
            operand[rel] = mean.astype(BF16)

    def project(chunk, q):
        cols = slice(q * piece, (q + 1) * piece)
        value = own_term[chunk, :, cols]
        for rel in range(REL):
            value += jnp.dot(operand[rel], weight_v[rel, :, cols], preferred_element_type=F32)
        return value

    def to_pair(i, q):
        return pltpu.make_async_remote_copy(
            src_ref=part.at[i, q], dst_ref=half_in.at[i, q],
            send_sem=pair_send.at[i, q], recv_sem=pair_recv.at[i, q],
            device_id=pair, device_id_type=MESH,
        )

    def to_far(q):
        return pltpu.make_async_remote_copy(
            src_ref=half_out.at[q], dst_ref=last_in.at[q],
            send_sem=far_send.at[q], recv_sem=far_recv.at[q],
            device_id=far, device_id_type=MESH,
        )

    def scale_to_far(q):
        return pltpu.make_async_remote_copy(
            src_ref=half_scale.at[q], dst_ref=last_scale.at[q],
            send_sem=scale_send.at[q], recv_sem=scale_recv.at[q],
            device_id=far, device_id_type=MESH,
        )

    def encode(q, value):
        top = jnp.maximum(jnp.max(jnp.abs(value), axis=1, keepdims=True), TINY)
        step = jnp.broadcast_to(top * (1.0 / LEVELS), (rows_out, BLK))
        half_scale[q] = jnp.transpose(step)[:1, :]
        half_out[q] = jnp.round(value * (LEVELS / top)).astype(jnp.int32).astype(jnp.int16)

    def decode(q):
        step = jnp.transpose(jnp.broadcast_to(last_scale[q], (BLK, rows_out)))
        step = jnp.concatenate([step] * (piece // BLK), axis=1)
        return last_in[q].astype(jnp.int32).astype(F32) * step

    chunk = (1 - high) * 2 + 1 - low
    operands(chunk)
    for q in range(COL_PIECES):
        part[0, q] = project(chunk, q)
        to_pair(0, q).start()

    chunk = (1 - high) * 2 + low
    operands(chunk)
    for q in range(COL_PIECES):
        value = project(chunk, q)
        to_pair(0, q).wait_recv()
        encode(q, value + half_in[0, q])
        scale_to_far(q).start()
        to_far(q).start()

    chunk = high * 2 + 1 - low
    operands(chunk)
    for q in range(COL_PIECES):
        part[1, q] = project(chunk, q)
        to_pair(1, q).start()

    chunk = high * 2 + low
    operands(chunk)
    for q in range(COL_PIECES):
        cols = slice(q * piece, (q + 1) * piece)
        value = project(chunk, q)
        to_pair(1, q).wait_recv()
        own_term[chunk, :, cols] = value + half_in[1, q] + bias_ref[:, cols]

    total = jnp.zeros((rows_out, 1), F32)
    for q in range(COL_PIECES):
        cols = slice(q * piece, (q + 1) * piece)
        scale_to_far(q).wait_recv()
        to_far(q).wait_recv()
        act = jnp.maximum(own_term[chunk, :, cols] + decode(q), 0.0)
        acted[q] = act
        total += jnp.sum(act, axis=1, keepdims=True)
    mu = total / width
    spread = jnp.zeros((rows_out, 1), F32)
    for q in range(COL_PIECES):
        dev = acted[q] - mu
        spread += jnp.sum(dev * dev, axis=1, keepdims=True)
    scale = lax.rsqrt(spread / width + epsilon)
    for q in range(COL_PIECES):
        cols = slice(q * piece, (q + 1) * piece)
        dev = acted[q] - mu
        out_ref[:, cols] = (dev * scale * gain_ref[:, cols] + offset_ref[:, cols]).astype(BF16)

    @pl.loop(0, steps)
    def _(step):
        ask(step).wait_send()
        for k in range(SHARES):
            answer(step, k).wait_send()

    for q in range(COL_PIECES):
        to_pair(0, q).wait_send()
        to_pair(1, q).wait_send()
        scale_to_far(q).wait_send()
        to_far(q).wait_send()


def body(feats, req_rows, req_slots, block_count, rel_weight, bias, gain, offset):
    owners = lax.axis_size("row")
    ranks = lax.axis_size("feat")
    nodes, columns = feats.shape
    rels, _, width = rel_weight.shape
    asks = req_rows.shape[1] // owners
    steps = owners - 1
    rows_out = 640 // ranks
    piece = width // COL_PIECES
    share = asks // SHARES
    packed = share + share // 2
    dma = pltpu.SemaphoreType.DMA
    vmem = pl.BlockSpec(memory_space=pltpu.VMEM)
    hbm = pl.BlockSpec(memory_space=pl.ANY)
    return pl.pallas_call(
        functools.partial(kernel, owners),
        out_shape=jax.ShapeDtypeStruct((rows_out, width), BF16),
        in_specs=[hbm] * 8,
        out_specs=vmem,
        scratch_shapes=[
            pltpu.SMEM(block_count.shape, jnp.int32),
            pltpu.VMEM(req_slots.shape, jnp.int32),
            pltpu.VMEM((1, width), F32),
            pltpu.VMEM((1, width), F32),
            pltpu.VMEM((1, width), F32),
            dma((5,)),
            pltpu.SMEM((owners, 1, asks), jnp.int32),
            pltpu.VMEM((columns, nodes), BF16),
            pltpu.VMEM((nodes, columns), F32),
            pltpu.VMEM((rels, columns, width), BF16),
            pltpu.VMEM((share, columns), F32),
            pltpu.VMEM((steps, SHARES, packed, BLK), BF16),
            pltpu.VMEM((owners, SHARES, packed, BLK), BF16),
            pltpu.VMEM((2 * asks, 2 * BLK), BF16),
            pltpu.VMEM((ranks, REL, rows_out, 2 * BLK), F32),
            pltpu.VMEM((ranks, rows_out, width), F32),
            pltpu.VMEM((REL, rows_out, columns), BF16),
            pltpu.VMEM((2, COL_PIECES, rows_out, piece), F32),
            pltpu.VMEM((2, COL_PIECES, rows_out, piece), F32),
            pltpu.VMEM((COL_PIECES, rows_out, piece), jnp.int16),
            pltpu.VMEM((COL_PIECES, 1, rows_out), F32),
            pltpu.VMEM((COL_PIECES, rows_out, piece), jnp.int16),
            pltpu.VMEM((COL_PIECES, 1, rows_out), F32),
            pltpu.VMEM((COL_PIECES, rows_out, piece), F32),
            dma((steps,)), dma((steps,)), dma((FEAT_CHUNKS,)), dma, dma,
            dma((steps, SHARES)), dma((steps, SHARES)),
            dma((2, COL_PIECES)), dma((2, COL_PIECES)),
            dma((COL_PIECES,)), dma((COL_PIECES,)), dma((COL_PIECES,)), dma((COL_PIECES,)),
        ],
        compiler_params=pltpu.CompilerParams(
            collective_id=0, has_side_effects=True, vmem_limit_bytes=58 * 1024 * 1024
        ),
        name="rgcn",
    )(
        block_count, req_rows, req_slots, feats.T, rel_weight,
        bias.reshape(1, -1), gain.reshape(1, -1), offset.reshape(1, -1),
    )


def solution(mesh):
    return jax.shard_map(
        body,
        mesh=mesh,
        in_specs=(
            P(("dom", "row"), "feat"),
            P(("dom", "row"), None),
            P(("dom", "row"), None),
            P(("dom", "row"), None),
            P(None, "feat", None),
            P(),
            P(),
            P(),
        ),
        out_specs=P(("dom", "row", "feat"), None),
        check_vma=False,
    )
```
